512 devices in a mesh: ctx: 64 (over z_hi, x, y, core), head: 8 (over z_lo).
Axes of the slice: x: 4, y: 4, z: 16 (z_hi: 2, z_lo: 8; z = z_hi * 8 + z_lo), core: 2. Of those that a mesh axis runs over, the one named last changes fastest.
Arguments:
- query_rows: bfloat16 [32768, 4096], P('ctx', 'head'), may hold values from -32 to 32
- key_rows: bfloat16 [32768, 1024], P('ctx', 'head'), may hold values from -32 to 32
- value_rows: bfloat16 [32768, 1024], P('ctx', 'head'), may hold values from -6 to 6
- out_weight: bfloat16 [4096, 4096], P('head', 'ctx'), may hold values from -0.71875 to 0.71875
Outputs:
- attended: bfloat16 [32768, 4096], P('ctx', 'head')
The draws below stay inside these ranges and needn't reach their ends.
All inputs are finite; a program needn't handle non-finite values.
Results may differ from the reference program's by a relative error of at most 0.015.
Values may be sent and summed in bfloat16 or wider, within the bound.
A program may use at most 64 MiB of HBM per device.

```python
from functools import reduce
import jax
import jax.numpy as jnp
from jax import lax

D = 4096
QH = 32
KVH = 8
HD = 128
BLOCK = 512
TOKENS = 32768
N_HEAD = 8


def draw_key_rows(key, part):
    sample = jax.random.normal(jax.random.fold_in(key, 11), (TOKENS, KVH * HD), jnp.float32)
    sample = jnp.clip(sample, -6.0, 6.0)
    return sample.astype(jnp.bfloat16)


def draw_query_rows(key, part):
    sample = 2.0 * jax.random.normal(jax.random.fold_in(key, 12), (TOKENS, QH * HD), jnp.float32)
    sample = jnp.clip(sample, -12.0, 12.0)
    return sample.astype(jnp.bfloat16)


def steps_of(rng, extent, shards, smallest, top_value):
    def one(dim, parts):
        heights = jax.random.uniform(jax.random.fold_in(jax.random.fold_in(rng, 6), dim), (parts,), jnp.float32, smallest / len(shards), top_value / len(shards))
        return jnp.repeat(jnp.exp(heights), extent[dim] // parts).reshape((-1,) + (1,) * (len(extent) - dim - 1))

    loudness = one(*shards[0])
    for cut in shards[1:]:
        loudness = loudness * one(*cut)
    return loudness


def normal_values(stream_key, dims, scale, bound, split=(), held_as=jnp.bfloat16):
    level = steps_of(stream_key, dims, split, -0.22, 0.18) if split else 1.0
    values = jax.random.normal(stream_key, dims, jnp.float32) * scale * level
    return jnp.minimum(jnp.maximum(values, -bound), bound).astype(held_as)


def setup_inputs(seed: int = 0) -> dict:
    key_of = jax.random.split(jax.random.key(seed), 5)
    return {
        "query_rows": draw_query_rows(jax.random.fold_in(key_of[4], 71), 0),
        "key_rows": draw_key_rows(jax.random.fold_in(key_of[4], 71), 0),
        "value_rows": normal_values(key_of[2], (TOKENS, KVH * HD), 1.0, 6.0, ((0, 64), (1, 8))),
        "out_weight": normal_values(key_of[3], (QH * HD, D), 0.12, 0.71875, ((0, 8), (1, 64))),
    }


def block_stats(query, key_block, value_block):
    group = QH // KVH
    key_heads = jnp.repeat(key_block.astype(jnp.float32).reshape(BLOCK, KVH, HD), group, axis=1)
    value_heads = jnp.repeat(value_block.astype(jnp.float32).reshape(BLOCK, KVH, HD), group, axis=1)
    scores = jnp.einsum("qhd,khd->hqk", query, key_heads) * (HD ** -0.5)
    peak = jnp.max(scores, axis=-1)
    weights = jnp.exp(scores - peak[..., None])
    total = jnp.sum(weights, axis=-1)
    probs = weights.astype(jnp.bfloat16).astype(jnp.float32)
    partial_out = jnp.einsum("hqk,khd->hqd", probs, value_heads)
    return peak, total, partial_out


def reference(query_rows, key_rows, value_rows, out_weight):
    count_blocks = query_rows.shape[0] // BLOCK
    level_count = count_blocks.bit_length() - 1

    def attend_block(index):
        query = lax.dynamic_slice_in_dim(query_rows, index * BLOCK, BLOCK, 0)
        query = query.astype(jnp.float32).reshape(BLOCK, QH, HD)
        sources = [index] + [jnp.bitwise_xor(index, jnp.int32(1 << level)) for level in range(level_count)]
        pieces = []
        for source in sources:
            start = (source * BLOCK).astype(jnp.int32)
            key_block = lax.dynamic_slice_in_dim(key_rows, start, BLOCK, 0)
            value_block = lax.dynamic_slice_in_dim(value_rows, start, BLOCK, 0)
            pieces.append(block_stats(query, key_block, value_block))
        top = reduce(jnp.maximum, [piece[0] for piece in pieces])
        numer = sum(jnp.exp(piece[0] - top)[..., None] * piece[2] for piece in pieces)
        denom = sum(jnp.exp(piece[0] - top) * piece[1] for piece in pieces)
        hidden_block = (numer / denom[..., None]).transpose(1, 0, 2).reshape(BLOCK, QH * HD)
        return hidden_block.astype(jnp.bfloat16)

    hidden = lax.map(attend_block, jnp.arange(count_blocks, dtype=jnp.int32))
    hidden = hidden.reshape(query_rows.shape[0], QH * HD)
    width_group = QH * HD // N_HEAD
    mixed = jnp.zeros((query_rows.shape[0], D), jnp.float32)
    for group_index in range(N_HEAD):
        lower = group_index * width_group
        term = jnp.dot(hidden[:, lower:lower + width_group], out_weight[lower:lower + width_group],
                       preferred_element_type=jnp.float32)
        mixed = mixed + lax.optimization_barrier(term.astype(jnp.bfloat16)).astype(jnp.float32)
    return mixed.astype(jnp.bfloat16)
```

```python
import math

import jax
import jax.numpy as jnp
from jax import lax
from jax.experimental import pallas as pl
from jax.experimental.pallas import tpu as pltpu
from jax.sharding import PartitionSpec as P

HD = 128
BLOCK = 512
GROUP = 4
NH = 8
SCALE = HD ** (-0.5) * math.log2(math.e)
MESH = pl.DeviceIdType.MESH
BF = jnp.bfloat16
F32 = jnp.float32


def flip(c, bit):
    return c + bit * (1 - 2 * lax.rem(lax.div(c, bit), 2))


def kernel(
    q_ref, k_ref, v_ref, w_ref, o_ref,
    qt, kb, vb, m_s, l_s, acc, ht, w1, wg, buf, og,
    k_send, k_recv, v_send, v_recv,
    wz_sem, w1a_send, w1a_recv, w1b_send, w1b_recv, w1c_send, w1c_recv,
    a2_send, a2_recv, wga_send, wga_recv, wgb_send, wgb_recv, wgc_send, wgc_recv,
    c_send, c_recv,
):
    c = lax.axis_index("ctx")
    p = lax.axis_index("head")
    zh = lax.div(c, 32)
    x = lax.rem(lax.div(c, 8), 4)
    y = lax.rem(lax.div(c, 2), 4)
    core = lax.rem(c, 2)
    partners = [None] + [flip(c, b) for b in (1, 2, 8, 4, 16, 32)]

    def at_x(r):
        nx = lax.rem(x + (r + 4), 4)
        return {"ctx": c + 8 * (nx - x)}, nx

    def at_y(r):
        ny = lax.rem(y + (r + 4), 4)
        return {"ctx": c + 2 * (ny - y)}, ny

    barrier = pltpu.get_barrier_semaphore()
    peers = [{"ctx": partners[1]}, {"ctx": partners[6]}]
    peers += [at_x(r)[0] for r in (1, 2, 3)] + [at_y(r)[0] for r in (1, 2, 3)]
    peers += [{"head": lax.rem(p + r, NH)} for r in range(1, NH)]
    for peer in peers:
        pl.semaphore_signal(barrier, inc=1, device_id=peer, device_id_type=MESH)

    def remote(src, dst, send, recv, peer):
        return pltpu.make_async_remote_copy(
            src_ref=src, dst_ref=dst, send_sem=send, recv_sem=recv,
            device_id=peer, device_id_type=MESH,
        )

    for g in range(GROUP):
        for tile in range(2):
            rows = q_ref[tile * 256:(tile + 1) * 256, g * HD:(g + 1) * HD]
            qt[tile * GROUP + g] = rows.T
    kb[0] = k_ref[...]
    vb[0] = v_ref[...].T
    own_w = 4 * zh + x
    w1[own_w, y, core] = w_ref[...]
    m_s[...] = jnp.full(m_s.shape, -1e30, F32)
    l_s[...] = jnp.zeros(l_s.shape, F32)
    acc[...] = jnp.zeros(acc.shape, F32)

    def attend(j, low, high):
        def one(i, carry):
            s = jnp.dot(kb[j], qt[i], preferred_element_type=F32)
            old = m_s[i]
            top = jnp.maximum(old, jnp.max(s, axis=0, keepdims=True))
            weights = jnp.exp2((s - top) * SCALE)
            fade = jnp.exp2((old - top) * SCALE)
            m_s[i] = top
            l_s[i] = fade * l_s[i] + jnp.sum(weights, axis=0, keepdims=True)
            part = jnp.dot(vb[j], weights.astype(BF), preferred_element_type=F32)
            acc[i] = fade * acc[i] + part
            return carry

        lax.fori_loop(low, high, one, 0)

    attend(0, 0, 8)
    pl.semaphore_wait(barrier, len(peers))

    other_w = 4 * (1 - zh) + x
    far = {"ctx": partners[6]}
    wz = remote(w1.at[own_w, y, core], w1.at[own_w, y, core], wz_sem.at[0], wz_sem.at[1], far)
    wz.start()

    def kv_copies(j, peer):
        return (
            remote(kb.at[0], kb.at[j], k_send.at[j - 1], k_recv.at[j - 1], peer),
            remote(vb.at[0], vb.at[j], v_send.at[j - 1], v_recv.at[j - 1], peer),
        )

    kv = [None]
    for j in range(1, 7):
        kv.append(kv_copies(j, {"ctx": partners[j]}))
    for j in (6, 1, 2, 3, 4, 5):
        for copy in kv[j]:
            copy.start()

    def kv_wait(j):
        for copy in kv_copies(j, far):
            copy.wait_recv()

    def near(j, carry):
        kv_wait(j)
        attend(j, 0, 8)
        return carry

    half = [pl.ds(0, 256), pl.ds(256, 256)]

    def w1_one(which, h, nx, ny):
        d = 4 * (zh if which == 0 else 1 - zh) + nx
        return w1.at[d, ny, core, :, half[h]]

    def w1_line(which, h, n):
        z = zh if which == 0 else 1 - zh
        if h == 0:
            return w1.at[4 * z + n, :, core, :, half[h]]
        return w1.at[pl.ds(4 * z, 4), n, core, :, half[h]]

    def w1_plane(which, h, co):
        z = zh if which == 0 else 1 - zh
        return w1.at[pl.ds(4 * z, 4), :, co, :, half[h]]

    def wg_one(h, nx, ny):
        return wg.at[:, nx, ny, core, :, half[h]]

    def wg_line(h, n):
        if h == 0:
            return wg.at[:, n, :, core, :, half[h]]
        return wg.at[:, :, n, core, :, half[h]]

    def wg_plane(h, co):
        return wg.at[:, :, :, co, :, half[h]]

    def phase_a(one, send, recv, h):
        first = at_y if h == 0 else at_x
        out, arrive = [], []
        for r in (1, 2, 3):
            peer, _ = first(r)
            block = one(h, x, y)
            out.append(remote(block, block, send.at[r - 1], recv.at[r - 1], peer))
            _, n = first(-r)
            block = one(h, x, n) if h == 0 else one(h, n, y)
            arrive.append(remote(block, block, send.at[r - 1], recv.at[r - 1], peer))
        return out, arrive

    def phase_b(line, send, recv, h):
        second = at_x if h == 0 else at_y
        out, arrive = [], []
        for r in (1, 2, 3):
            peer, _ = second(r)
            block = line(h, x if h == 0 else y)
            out.append(remote(block, block, send.at[r - 1], recv.at[r - 1], peer))
            _, n = second(-r)
            block = line(h, n)
            arrive.append(remote(block, block, send.at[r - 1], recv.at[r - 1], peer))
        return out, arrive

    def phase_c(plane, send, recv, h):
        peer = {"ctx": partners[1]}
        block = plane(h, core)
        out = [remote(block, block, send, recv, peer)]
        block = plane(h, 1 - core)
        arrive = [remote(block, block, send, recv, peer)]
        return out, arrive

    def start(pair):
        for copy in pair[0]:
            copy.start()

    def arrived(pair):
        for copy in pair[1]:
            copy.wait_recv()

    def sent(pair):
        for copy in pair[0]:
            copy.wait_send()

    w1a, w1b, w1c = {}, {}, {}
    for which in range(2):
        for h in range(2):
            key = (which, h)
            w1a[key] = phase_a(
                lambda hh, nx, ny, which=which: w1_one(which, hh, nx, ny),
                w1a_send.at[which, h], w1a_recv.at[which, h], h)
            w1b[key] = phase_b(
                lambda hh, n, which=which: w1_line(which, hh, n),
                w1b_send.at[which, h], w1b_recv.at[which, h], h)
            w1c[key] = phase_c(
                lambda hh, co, which=which: w1_plane(which, hh, co),
                w1c_send.at[which, h], w1c_recv.at[which, h], h)
    wga = [phase_a(wg_one, wga_send.at[h], wga_recv.at[h], h) for h in range(2)]
    wgb = [phase_b(wg_line, wgb_send.at[h], wgb_recv.at[h], h) for h in range(2)]
    wgc = [phase_c(wg_plane, wgc_send.at[h], wgc_recv.at[h], h) for h in range(2)]

    for h in range(2):
        start(w1a[0, h])
    lax.fori_loop(1, 4, near, 0)
    for h in range(2):
        arrived(w1a[0, h])
        start(w1b[0, h])
    remote(w1.at[other_w, y, core], w1.at[other_w, y, core], wz_sem.at[0], wz_sem.at[1], far).wait_recv()
    for h in range(2):
        start(w1a[1, h])
    lax.fori_loop(4, 6, near, 0)
    for h in range(2):
        arrived(w1a[1, h])
        start(w1b[1, h])
    for h in range(2):
        arrived(w1b[0, h])
        start(w1c[0, h])
    for h in range(2):
        arrived(w1b[1, h])
        start(w1c[1, h])

    right = {"head": lax.rem(p + 1, NH)}
    left = {"head": lax.rem(p + NH - 1, NH)}

    def chain(way, k, q, src):
        return remote(src, buf.at[way, k, q], c_send.at[way, k, q], c_recv.at[way, k, q],
                      right if way == 0 else left)

    has_up = (p > 0, p < NH - 1)
    has_down = (p < NH - 1, p > 0)
    place = (p, NH - 1 - p)

    def finish(tile):
        for g in range(GROUP):
            i = tile * GROUP + g
            value = (acc[i] / l_s[i]).astype(BF)
            for q in range(2):
                ht[tile * 2 + q, g * HD:(g + 1) * HD, :] = value[:, q * 128:(q + 1) * 128]

    kv_wait(6)
    attend(6, 0, 4)
    finish(0)
    for q in range(2):
        for way in range(2):
            @pl.when(has_down[way])
            def _():
                chain(way, 0, q, ht.at[q]).start()
    attend(6, 4, 8)
    finish(1)
    for which in range(2):
        for h in range(2):
            arrived(w1c[which, h])

    u = x * 8 + y * 2 + core
    uy, uc, uo = lax.div(u, 8), lax.rem(lax.div(u, 4), 2), lax.rem(u, 4) * 16
    wg[p, x, y, core] = w1[p, uy, uc, pl.ds(pl.multiple_of(uo, 16), 16)]

    def a2(r):
        d = lax.rem(p + r, NH)
        return remote(
            w1.at[d, uy, uc, pl.ds(pl.multiple_of(uo, 16), 16)], wg.at[p, x, y, core],
            a2_send.at[r - 1], a2_recv.at[r - 1], {"head": d})

    for r in range(1, NH):
        a2(r).start()

    def term(d, q):
        return jnp.dot(w1[d].reshape(512, 512), ht[2 + q], preferred_element_type=F32)

    def step(k, carry):
        for q in range(2):
            for way in range(2):
                slot = buf.at[way, k - 1, q]

                @pl.when(has_up[way])
                def _():
                    chain(way, k - 1, q, slot).wait_recv()

                adds = jnp.logical_and(k > place[way], has_down[way])
                far_place = NH + place[way] - k
                d = far_place if way == 0 else NH - 1 - far_place

                @pl.when(jnp.logical_and(adds, has_up[way]))
                def _():
                    slot[...] = (slot[...].astype(F32) + term(d, q)).astype(BF)

                @pl.when(jnp.logical_and(adds, jnp.logical_not(has_up[way])))
                def _():
                    slot[...] = term(d, q).astype(BF)

                @pl.when(has_down[way])
                def _():
                    chain(way, k - 1, q, slot).wait_send()
                    chain(way, k, q, slot).start()
        return carry

    lax.fori_loop(1, 3, step, 0)
    for r in range(1, NH):
        h = lax.rem(p + (NH - r), NH)
        block = wg.at[h, x, y, core]
        remote(block, block, a2_send.at[r - 1], a2_recv.at[r - 1], right).wait_recv()
    for h in range(2):
        start(wga[h])
    lax.fori_loop(3, 4, step, 0)
    for h in range(2):
        arrived(wga[h])
        start(wgb[h])
    lax.fori_loop(4, 6, step, 0)
    for h in range(2):
        arrived(wgb[h])
        start(wgc[h])
    lax.fori_loop(6, 8, step, 0)

    for h in range(2):
        arrived(wgc[h])
    for q in range(2):
        og[q] = jnp.dot(wg[p].reshape(512, 512), ht[q], preferred_element_type=F32)

    def gathered(h, carry):
        for q in range(2):
            @pl.when(h < p)
            def _():
                og[q] += jnp.dot(wg[h].reshape(512, 512), buf[0, p - 1 - h, q], preferred_element_type=F32)

            @pl.when(h > p)
            def _():
                og[q] += jnp.dot(wg[h].reshape(512, 512), buf[1, h - p - 1, q], preferred_element_type=F32)
        return carry

    lax.fori_loop(0, NH, gathered, 0)
    for q in range(2):
        o_ref[q * 128:(q + 1) * 128, :] = og[q].T.astype(BF)
    for q in range(2):
        og[q] = term(p, q)
    for q in range(2):
        for way in range(2):
            @pl.when(has_up[way])
            def _():
                chain(way, NH - 1, q, ht.at[q]).wait_recv()
                og[q] += buf[way, NH - 1, q].astype(F32)
        o_ref[256 + q * 128:256 + (q + 1) * 128, :] = og[q].T.astype(BF)

    for q in range(2):
        for way in range(2):
            @pl.when(has_down[way])
            def _():
                chain(way, NH - 1, q, ht.at[q]).wait_send()
    wz.wait_send()
    for j in range(1, 7):
        for copy in kv[j]:
            copy.wait_send()
    for which in range(2):
        for h in range(2):
            sent(w1a[which, h])
            sent(w1b[which, h])
            sent(w1c[which, h])
    for r in range(1, NH):
        a2(r).wait_send()
    for h in range(2):
        sent(wga[h])
        sent(wgb[h])
        sent(wgc[h])


def shards(query_rows, key_rows, value_rows, out_weight):
    dma = pltpu.SemaphoreType.DMA
    vmem = pl.BlockSpec(memory_space=pltpu.VMEM)
    return pl.pallas_call(
        kernel,
        out_shape=jax.ShapeDtypeStruct((BLOCK, GROUP * HD), BF),
        in_specs=[vmem] * 4,
        out_specs=vmem,
        scratch_shapes=[
            pltpu.VMEM((8, HD, 256), BF),
            pltpu.VMEM((7, BLOCK, HD), BF),
            pltpu.VMEM((7, HD, BLOCK), BF),
            pltpu.VMEM((8, 1, 256), F32),
            pltpu.VMEM((8, 1, 256), F32),
            pltpu.VMEM((8, HD, 256), F32),
            pltpu.VMEM((4, 512, 128), BF),
            pltpu.VMEM((8, 4, 2, 64, 512), BF),
            pltpu.VMEM((8, 4, 4, 2, 16, 512), BF),
            pltpu.VMEM((2, 8, 2, 512, 128), BF),
            pltpu.VMEM((2, 512, 128), F32),
            dma((6,)), dma((6,)), dma((6,)), dma((6,)),
            dma((2,)),
            dma((2, 2, 3)), dma((2, 2, 3)), dma((2, 2, 3)), dma((2, 2, 3)), dma((2, 2)), dma((2, 2)),
            dma((7,)), dma((7,)),
            dma((2, 3)), dma((2, 3)), dma((2, 3)), dma((2, 3)), dma((2,)), dma((2,)),
            dma((2, 8, 2)), dma((2, 8, 2)),
        ],
        compiler_params=pltpu.CompilerParams(
            collective_id=0, has_side_effects=True, vmem_limit_bytes=48 * 1024 * 1024
        ),
        cost_estimate=pl.CostEstimate(flops=6_000_000_000, bytes_accessed=2_000_000, transcendentals=7_400_000),
    )(query_rows, key_rows, value_rows, out_weight.T)


def solution(mesh):
    placed = (P("ctx", "head"), P("ctx", "head"), P("ctx", "head"), P("head", "ctx"))
    return jax.shard_map(
        shards, mesh=mesh, in_specs=placed, out_specs=P("ctx", "head"), check_vma=False
    )
```

```python
import math

import jax
import jax.numpy as jnp
from jax import lax
from jax.experimental import pallas as pl
from jax.experimental.pallas import tpu as pltpu
from jax.sharding import PartitionSpec as P

HD = 128
BLOCK = 512
GROUP = 4
NH = 8
SCALE = HD ** (-0.5) * math.log2(math.e)
MESH = pl.DeviceIdType.MESH
BF = jnp.bfloat16
F32 = jnp.float32


def flip(c, bit):
    return c + bit * (1 - 2 * lax.rem(lax.div(c, bit), 2))


def kernel(
    q_hbm, k_hbm, v_hbm, w_hbm, o_ref,
    q_ref, v_ref, qt, kb, vb, m_s, l_s, acc, ht, w1, wg, buf, og, in_sem,
    k_send, k_recv, v_send, v_recv,
    wz_sem, w1a_send, w1a_recv, w1b_send, w1b_recv, w1c_send, w1c_recv,
    a2_send, a2_recv, wga_send, wga_recv, wgb_send, wgb_recv, wgc_send, wgc_recv,
    c_send, c_recv,
):
    c = lax.axis_index("ctx")
    p = lax.axis_index("head")
    zh = lax.div(c, 32)
    x = lax.rem(lax.div(c, 8), 4)
    y = lax.rem(lax.div(c, 2), 4)
    core = lax.rem(c, 2)
    partners = [None] + [flip(c, b) for b in (1, 2, 8, 4, 16, 32)]

    def at_x(r):
        nx = lax.rem(x + (r + 4), 4)
        return {"ctx": c + 8 * (nx - x)}, nx

    def at_y(r):
        ny = lax.rem(y + (r + 4), 4)
        return {"ctx": c + 2 * (ny - y)}, ny

    barrier = pltpu.get_barrier_semaphore()
    peers = [{"ctx": partners[1]}, {"ctx": partners[6]}]
    peers += [at_x(r)[0] for r in (1, 2, 3)] + [at_y(r)[0] for r in (1, 2, 3)]
    ring = (1, 2, 3, 4, -1, -2, -3)

    def at_z(r):
        z = lax.rem(8 * zh + p + (r + 16), 16)
        return {"ctx": c + 32 * (lax.div(z, 8) - zh), "head": lax.rem(z, 8)}, lax.rem(z, 8)

    peers += [at_z(-r)[0] for r in ring]
    for peer in peers:
        pl.semaphore_signal(barrier, inc=1, device_id=peer, device_id_type=MESH)

    def remote(src, dst, send, recv, peer):
        return pltpu.make_async_remote_copy(
            src_ref=src, dst_ref=dst, send_sem=send, recv_sem=recv,
            device_id=peer, device_id_type=MESH,
        )

    own_w = 4 * zh + x
    loads = [
        pltpu.make_async_copy(v_hbm, v_ref, in_sem.at[0]),
        pltpu.make_async_copy(k_hbm, kb.at[0], in_sem.at[1]),
        pltpu.make_async_copy(q_hbm, q_ref, in_sem.at[2]),
        pltpu.make_async_copy(w_hbm, w1.at[own_w, y, core], in_sem.at[3]),
    ]
    for copy in loads:
        copy.start()
    m_s[...] = jnp.full(m_s.shape, -1e30, F32)
    l_s[...] = jnp.zeros(l_s.shape, F32)
    acc[...] = jnp.zeros(acc.shape, F32)
    loads[0].wait()
    vb[0] = v_ref[...].T
    loads[1].wait()
    loads[2].wait()
    for g in range(GROUP):
        for tile in range(2):
            rows = q_ref[tile * 256:(tile + 1) * 256, g * HD:(g + 1) * HD]
            qt[tile * GROUP + g] = rows.T
    loads[3].wait()

    def attend(j, tile):
        part = range(tile * GROUP, (tile + 1) * GROUP)
        scores = [jnp.dot(kb[j], qt[i], preferred_element_type=F32) for i in part]
        old = [m_s[i] for i in part]
        top = [jnp.maximum(o, jnp.max(s, axis=0, keepdims=True)) for o, s in zip(old, scores)]
        weights = [jnp.exp2((s - t) * SCALE) for s, t in zip(scores, top)]
        fade = [jnp.exp2((o - t) * SCALE) for o, t in zip(old, top)]
        total = [f * l_s[i] + jnp.sum(w, axis=0, keepdims=True) for f, i, w in zip(fade, part, weights)]
        output = [
            f * acc[i] + jnp.dot(vb[j], w.astype(BF), preferred_element_type=F32)
            for f, i, w in zip(fade, part, weights)
        ]
        for n, i in enumerate(part):
            m_s[i] = top[n]
            l_s[i] = total[n]
            acc[i] = output[n]

    attend(0, 0)
    attend(0, 1)
    pl.semaphore_wait(barrier, len(peers))

    other_w = 4 * (1 - zh) + x
    far = {"ctx": partners[6]}
    wz = remote(w1.at[own_w, y, core], w1.at[own_w, y, core], wz_sem.at[0], wz_sem.at[1], far)
    wz.start()

    def kv_copies(j, peer):
        return (
            remote(kb.at[0], kb.at[j], k_send.at[j - 1], k_recv.at[j - 1], peer),
            remote(vb.at[0], vb.at[j], v_send.at[j - 1], v_recv.at[j - 1], peer),
        )

    kv = [None]
    for j in range(1, 7):
        kv.append(kv_copies(j, {"ctx": partners[j]}))
    for j in (6, 1):
        for copy in kv[j]:
            copy.start()

    def kv_wait(j):
        for copy in kv_copies(j, far):
            copy.wait_recv()

    def near(j, carry):
        kv_wait(j)
        attend(j, 0)
        attend(j, 1)
        return carry

    half = [pl.ds(0, 256), pl.ds(256, 256)]

    def w1_one(which, h, nx, ny):
        d = 4 * (zh if which == 0 else 1 - zh) + nx
        return w1.at[d, ny, core, :, half[h]]

    def w1_line(which, h, n):
        z = zh if which == 0 else 1 - zh
        if h == 0:
            return w1.at[4 * z + n, :, core, :, half[h]]
        return w1.at[pl.ds(4 * z, 4), n, core, :, half[h]]

    def w1_plane(which, h, co):
        z = zh if which == 0 else 1 - zh
        return w1.at[pl.ds(4 * z, 4), :, co, :, half[h]]

    def wg_one(h, nx, ny):
        return wg.at[:, nx, ny, core, :, half[h]]

    def wg_line(h, n):
        if h == 0:
            return wg.at[:, n, :, core, :, half[h]]
        return wg.at[:, :, n, core, :, half[h]]

    def wg_plane(h, co):
        return wg.at[:, :, :, co, :, half[h]]

    def phase_a(one, send, recv, h):
        first = at_y if h == 0 else at_x
        out, arrive = [], []
        for r in (1, 2, 3):
            peer, _ = first(r)
            block = one(h, x, y)
            out.append(remote(block, block, send.at[r - 1], recv.at[r - 1], peer))
            _, n = first(-r)
            block = one(h, x, n) if h == 0 else one(h, n, y)
            arrive.append(remote(block, block, send.at[r - 1], recv.at[r - 1], peer))
        return out, arrive

    def phase_b(line, send, recv, h):
        second = at_x if h == 0 else at_y
        out, arrive = [], []
        for r in (1, 2, 3):
            peer, _ = second(r)
            block = line(h, x if h == 0 else y)
            out.append(remote(block, block, send.at[r - 1], recv.at[r - 1], peer))
            _, n = second(-r)
            block = line(h, n)
            arrive.append(remote(block, block, send.at[r - 1], recv.at[r - 1], peer))
        return out, arrive

    def phase_c(plane, send, recv, h):
        peer = {"ctx": partners[1]}
        block = plane(h, core)
        out = [remote(block, block, send, recv, peer)]
        block = plane(h, 1 - core)
        arrive = [remote(block, block, send, recv, peer)]
        return out, arrive

    def start(pair):
        for copy in pair[0]:
            copy.start()

    def arrived(pair):
        for copy in pair[1]:
            copy.wait_recv()

    def sent(pair):
        for copy in pair[0]:
            copy.wait_send()

    w1a, w1b, w1c = {}, {}, {}
    for which in range(2):
        for h in range(2):
            key = (which, h)
            w1a[key] = phase_a(
                lambda hh, nx, ny, which=which: w1_one(which, hh, nx, ny),
                w1a_send.at[which, h], w1a_recv.at[which, h], h)
            w1b[key] = phase_b(
                lambda hh, n, which=which: w1_line(which, hh, n),
                w1b_send.at[which, h], w1b_recv.at[which, h], h)
            w1c[key] = phase_c(
                lambda hh, co, which=which: w1_plane(which, hh, co),
                w1c_send.at[which, h], w1c_recv.at[which, h], h)
    wga = [phase_a(wg_one, wga_send.at[h], wga_recv.at[h], h) for h in range(2)]
    wgb = [phase_b(wg_line, wgb_send.at[h], wgb_recv.at[h], h) for h in range(2)]
    wgc = [phase_c(wg_plane, wgc_send.at[h], wgc_recv.at[h], h) for h in range(2)]

    for h in range(2):
        start(w1a[0, h])
    for j in range(2, 6):
        for copy in kv[j]:
            copy.start()
    lax.fori_loop(1, 2, near, 0)
    for h in range(2):
        arrived(w1a[0, h])
        start(w1b[0, h])
    remote(w1.at[other_w, y, core], w1.at[other_w, y, core], wz_sem.at[0], wz_sem.at[1], far).wait_recv()
    for h in range(2):
        start(w1a[1, h])
    lax.fori_loop(2, 3, near, 0)
    for h in range(2):
        arrived(w1a[1, h])
        start(w1b[1, h])
    lax.fori_loop(3, 6, near, 0)
    for h in range(2):
        arrived(w1b[0, h])
        start(w1c[0, h])
    for h in range(2):
        arrived(w1b[1, h])
        start(w1c[1, h])

    right = {"head": lax.rem(p + 1, NH)}
    left = {"head": lax.rem(p + NH - 1, NH)}

    def chain(way, k, q, src):
        return remote(src, buf.at[way, k, q], c_send.at[way, k, q], c_recv.at[way, k, q],
                      right if way == 0 else left)

    has_up = (p > 0, p < NH - 1)
    has_down = (p < NH - 1, p > 0)
    place = (p, NH - 1 - p)

    def finish(tile):
        for g in range(GROUP):
            i = tile * GROUP + g
            value = (acc[i] / l_s[i]).astype(BF)
            for q in range(2):
                ht[tile * 2 + q, g * HD:(g + 1) * HD, :] = value[:, q * 128:(q + 1) * 128]

    for which in range(2):
        for h in range(2):
            arrived(w1c[which, h])
    u = x * 8 + y * 2 + core
    uy, uc, uo = lax.div(u, 8), lax.rem(lax.div(u, 4), 2), lax.rem(u, 4) * 16
    wg[p, x, y, core] = w1[p, uy, uc, pl.ds(pl.multiple_of(uo, 16), 16)]

    def a2(n):
        peer, d = at_z(ring[n])
        return remote(
            w1.at[d, uy, uc, pl.ds(pl.multiple_of(uo, 16), 16)], wg.at[p, x, y, core],
            a2_send.at[n], a2_recv.at[n], peer)

    for n in range(len(ring)):
        a2(n).start()

    kv_wait(6)
    attend(6, 0)
    finish(0)
    for q in range(2):
        for way in range(2):
            @pl.when(has_down[way])
            def _():
                chain(way, 0, q, ht.at[q]).start()
    attend(6, 1)
    finish(1)

    def term(d, q):
        return jnp.dot(w1[d].reshape(512, 512), ht[2 + q], preferred_element_type=F32)

    def step(k, carry):
        for q in range(2):
            for way in range(2):
                slot = buf.at[way, k - 1, q]

                @pl.when(has_up[way])
                def _():
                    chain(way, k - 1, q, slot).wait_recv()

                adds = jnp.logical_and(k > place[way], has_down[way])
                far_place = NH + place[way] - k
                d = far_place if way == 0 else NH - 1 - far_place

                @pl.when(jnp.logical_and(adds, has_up[way]))
                def _():
                    slot[...] = (slot[...].astype(F32) + term(d, q)).astype(BF)

                @pl.when(jnp.logical_and(adds, jnp.logical_not(has_up[way])))
                def _():
                    slot[...] = term(d, q).astype(BF)

                @pl.when(has_down[way])
                def _():
                    chain(way, k - 1, q, slot).wait_send()
                    chain(way, k, q, slot).start()
        return carry

    lax.fori_loop(1, 3, step, 0)
    for n in range(len(ring)):
        block = wg.at[at_z(-ring[n])[1], x, y, core]
        remote(block, block, a2_send.at[n], a2_recv.at[n], right).wait_recv()
    for h in range(2):
        start(wga[h])
    lax.fori_loop(3, 4, step, 0)
    for h in range(2):
        arrived(wga[h])
        start(wgb[h])
    lax.fori_loop(4, 6, step, 0)
    for h in range(2):
        arrived(wgb[h])
        start(wgc[h])
    lax.fori_loop(6, 8, step, 0)

    for h in range(2):
        arrived(wgc[h])
    for q in range(2):
        og[q] = jnp.dot(wg[p].reshape(512, 512), ht[q], preferred_element_type=F32)

    def gathered(h, carry):
        for q in range(2):
            @pl.when(h < p)
            def _():
                og[q] += jnp.dot(wg[h].reshape(512, 512), buf[0, p - 1 - h, q], preferred_element_type=F32)

            @pl.when(h > p)
            def _():
                og[q] += jnp.dot(wg[h].reshape(512, 512), buf[1, h - p - 1, q], preferred_element_type=F32)
        return carry

    lax.fori_loop(0, NH, gathered, 0)
    for q in range(2):
        o_ref[q * 128:(q + 1) * 128, :] = og[q].T.astype(BF)
    for q in range(2):
        og[q] = term(p, q)
    for q in range(2):
        for way in range(2):
            @pl.when(has_up[way])
            def _():
                chain(way, NH - 1, q, ht.at[q]).wait_recv()
                og[q] += buf[way, NH - 1, q].astype(F32)
        o_ref[256 + q * 128:256 + (q + 1) * 128, :] = og[q].T.astype(BF)

    for q in range(2):
        for way in range(2):
            @pl.when(has_down[way])
            def _():
                chain(way, NH - 1, q, ht.at[q]).wait_send()
    wz.wait_send()
    for j in range(1, 7):
        for copy in kv[j]:
            copy.wait_send()
    for which in range(2):
        for h in range(2):
            sent(w1a[which, h])
            sent(w1b[which, h])
            sent(w1c[which, h])
    for n in range(len(ring)):
        a2(n).wait_send()
    for h in range(2):
        sent(wga[h])
        sent(wgb[h])
        sent(wgc[h])


def shards(query_rows, key_rows, value_rows, out_weight):
    dma = pltpu.SemaphoreType.DMA
    vmem = pl.BlockSpec(memory_space=pltpu.VMEM)
    return pl.pallas_call(
        kernel,
        out_shape=jax.ShapeDtypeStruct((BLOCK, GROUP * HD), BF),
        in_specs=[pl.BlockSpec(memory_space=pltpu.HBM)] * 4,
        out_specs=vmem,
        scratch_shapes=[
            pltpu.VMEM((BLOCK, GROUP * HD), BF),
            pltpu.VMEM((BLOCK, HD), BF),
            pltpu.VMEM((8, HD, 256), BF),
            pltpu.VMEM((7, BLOCK, HD), BF),
            pltpu.VMEM((7, HD, BLOCK), BF),
            pltpu.VMEM((8, 1, 256), F32),
            pltpu.VMEM((8, 1, 256), F32),
            pltpu.VMEM((8, HD, 256), F32),
            pltpu.VMEM((4, 512, 128), BF),
            pltpu.VMEM((8, 4, 2, 64, 512), BF),
            pltpu.VMEM((8, 4, 4, 2, 16, 512), BF),
            pltpu.VMEM((2, 8, 2, 512, 128), BF),
            pltpu.VMEM((2, 512, 128), F32),
            dma((4,)),
            dma((6,)), dma((6,)), dma((6,)), dma((6,)),
            dma((2,)),
            dma((2, 2, 3)), dma((2, 2, 3)), dma((2, 2, 3)), dma((2, 2, 3)), dma((2, 2)), dma((2, 2)),
            dma((7,)), dma((7,)),
            dma((2, 3)), dma((2, 3)), dma((2, 3)), dma((2, 3)), dma((2,)), dma((2,)),
            dma((2, 8, 2)), dma((2, 8, 2)),
        ],
        compiler_params=pltpu.CompilerParams(
            collective_id=0, has_side_effects=True, vmem_limit_bytes=60 * 1024 * 1024
        ),
        cost_estimate=pl.CostEstimate(flops=6_000_000_000, bytes_accessed=2_000_000, transcendentals=7_400_000),
    )(query_rows, key_rows, value_rows, out_weight.T)


def solution(mesh):
    placed = (P("ctx", "head"), P("ctx", "head"), P("ctx", "head"), P("head", "ctx"))
    return jax.shard_map(
        shards, mesh=mesh, in_specs=placed, out_specs=P("ctx", "head"), check_vma=False
    )
```

```python
import math

import jax
import jax.numpy as jnp
from jax import lax
from jax.experimental import pallas as pl
from jax.experimental.pallas import tpu as pltpu
from jax.sharding import PartitionSpec as P

HD = 128
BLOCK = 512
GROUP = 4
NH = 8
SCALE = HD ** (-0.5) * math.log2(math.e)
MESH = pl.DeviceIdType.MESH
BF = jnp.bfloat16
F32 = jnp.float32


def flip(c, bit):
    return c + bit * (1 - 2 * lax.rem(lax.div(c, bit), 2))


def kernel(
    q_hbm, k_hbm, v_hbm, w_hbm, o_ref,
    q_ref, v_ref, qt, kb, vb, m_s, l_s, acc, ht, w1, wg, buf, og, in_sem,
    k_send, k_recv, v_send, v_recv,
    wz_sem, w1a_send, w1a_recv, w1b_send, w1b_recv, w1c_send, w1c_recv,
    a2_send, a2_recv, wga_send, wga_recv, wgb_send, wgb_recv, wgc_send, wgc_recv,
    c_send, c_recv,
):
    c = lax.axis_index("ctx")
    p = lax.axis_index("head")
    zh = lax.div(c, 32)
    x = lax.rem(lax.div(c, 8), 4)
    y = lax.rem(lax.div(c, 2), 4)
    core = lax.rem(c, 2)
    partners = [None] + [flip(c, b) for b in (1, 2, 8, 4, 16, 32)]

    def at_x(r):
        nx = lax.rem(x + (r + 4), 4)
        return {"ctx": c + 8 * (nx - x)}, nx

    def at_y(r):
        ny = lax.rem(y + (r + 4), 4)
        return {"ctx": c + 2 * (ny - y)}, ny

    barrier = pltpu.get_barrier_semaphore()
    peers = [{"ctx": partners[1]}, {"ctx": partners[6]}]
    peers += [at_x(r)[0] for r in (1, 2, 3)] + [at_y(r)[0] for r in (1, 2, 3)]
    ring = (1, 2, 3, 4, -1, -2, -3)

    def at_z(r):
        z = lax.rem(8 * zh + p + (r + 16), 16)
        return {"ctx": c + 32 * (lax.div(z, 8) - zh), "head": lax.rem(z, 8)}, lax.rem(z, 8)

    peers += [at_z(-r)[0] for r in ring]
    for peer in peers:
        pl.semaphore_signal(barrier, inc=1, device_id=peer, device_id_type=MESH)

    def remote(src, dst, send, recv, peer):
        return pltpu.make_async_remote_copy(
            src_ref=src, dst_ref=dst, send_sem=send, recv_sem=recv,
            device_id=peer, device_id_type=MESH,
        )

    own_w = 4 * zh + x
    loads = [
        pltpu.make_async_copy(v_hbm, v_ref, in_sem.at[0]),
        pltpu.make_async_copy(k_hbm, kb.at[0], in_sem.at[1]),
        pltpu.make_async_copy(q_hbm, q_ref, in_sem.at[2]),
        pltpu.make_async_copy(w_hbm, w1.at[own_w, y, core], in_sem.at[3]),
    ]
    for copy in loads:
        copy.start()
    m_s[...] = jnp.full(m_s.shape, -1e30, F32)
    l_s[...] = jnp.zeros(l_s.shape, F32)
    acc[...] = jnp.zeros(acc.shape, F32)
    loads[0].wait()
    vb[0] = v_ref[...].T
    loads[1].wait()
    loads[2].wait()
    for g in range(GROUP):
        for tile in range(2):
            rows = q_ref[tile * 256:(tile + 1) * 256, g * HD:(g + 1) * HD]
            qt[tile * GROUP + g] = rows.T
    loads[3].wait()

    def attend(j, tile):
        part = range(tile * GROUP, (tile + 1) * GROUP)
        scores = [jnp.dot(kb[j], qt[i], preferred_element_type=F32) for i in part]
        old = [m_s[i] for i in part]
        top = [jnp.maximum(o, jnp.max(s, axis=0, keepdims=True)) for o, s in zip(old, scores)]
        weights = [jnp.exp2((s - t) * SCALE) for s, t in zip(scores, top)]
        fade = [jnp.exp2((o - t) * SCALE) for o, t in zip(old, top)]
        total = [f * l_s[i] + jnp.sum(w, axis=0, keepdims=True) for f, i, w in zip(fade, part, weights)]
        output = [
            f * acc[i] + jnp.dot(vb[j], w.astype(BF), preferred_element_type=F32)
            for f, i, w in zip(fade, part, weights)
        ]
        for n, i in enumerate(part):
            m_s[i] = top[n]
            l_s[i] = total[n]
            acc[i] = output[n]

    attend(0, 0)
    attend(0, 1)
    pl.semaphore_wait(barrier, len(peers))

    other_w = 4 * (1 - zh) + x
    far = {"ctx": partners[6]}
    wz = remote(w1.at[own_w, y, core], w1.at[own_w, y, core], wz_sem.at[0], wz_sem.at[1], far)
    wz.start()

    def kv_copies(j, peer):
        return (
            remote(kb.at[0], kb.at[j], k_send.at[j - 1], k_recv.at[j - 1], peer),
            remote(vb.at[0], vb.at[j], v_send.at[j - 1], v_recv.at[j - 1], peer),
        )

    kv = [None]
    for j in range(1, 7):
        kv.append(kv_copies(j, {"ctx": partners[j]}))
    for j in (6, 1):
        for copy in kv[j]:
            copy.start()

    def kv_wait(j):
        for copy in kv_copies(j, far):
            copy.wait_recv()

    def near(j, carry):
        kv_wait(j)
        attend(j, 0)
        attend(j, 1)
        return carry

    half = [pl.ds(0, 256), pl.ds(256, 256)]

    def w1_one(which, h, nx, ny):
        d = 4 * (zh if which == 0 else 1 - zh) + nx
        return w1.at[d, ny, core, :, half[h]]

    def w1_line(which, h, n):
        z = zh if which == 0 else 1 - zh
        if h == 0:
            return w1.at[4 * z + n, :, core, :, half[h]]
        return w1.at[pl.ds(4 * z, 4), n, core, :, half[h]]

    def w1_plane(which, h, co):
        z = zh if which == 0 else 1 - zh
        return w1.at[pl.ds(4 * z, 4), :, co, :, half[h]]

    def wg_one(h, nx, ny):
        return wg.at[:, nx, ny, core, :, half[h]]

    def wg_line(h, n):
        if h == 0:
            return wg.at[:, n, :, core, :, half[h]]
        return wg.at[:, :, n, core, :, half[h]]

    def wg_plane(h, co):
        return wg.at[:, :, :, co, :, half[h]]

    def phase_a(one, send, recv, h):
        first = at_y if h == 0 else at_x
        out, arrive = [], []
        for r in (1, 2, 3):
            peer, _ = first(r)
            block = one(h, x, y)
            out.append(remote(block, block, send.at[r - 1], recv.at[r - 1], peer))
            _, n = first(-r)
            block = one(h, x, n) if h == 0 else one(h, n, y)
            arrive.append(remote(block, block, send.at[r - 1], recv.at[r - 1], peer))
        return out, arrive

    def phase_b(line, send, recv, h):
        second = at_x if h == 0 else at_y
        out, arrive = [], []
        for r in (1, 2, 3):
            peer, _ = second(r)
            block = line(h, x if h == 0 else y)
            out.append(remote(block, block, send.at[r - 1], recv.at[r - 1], peer))
            _, n = second(-r)
            block = line(h, n)
            arrive.append(remote(block, block, send.at[r - 1], recv.at[r - 1], peer))
        return out, arrive

    def phase_c(plane, send, recv, h):
        peer = {"ctx": partners[1]}
        block = plane(h, core)
        out = [remote(block, block, send, recv, peer)]
        block = plane(h, 1 - core)
        arrive = [remote(block, block, send, recv, peer)]
        return out, arrive

    def start(pair):
        for copy in pair[0]:
            copy.start()

    def arrived(pair):
        for copy in pair[1]:
            copy.wait_recv()

    def sent(pair):
        for copy in pair[0]:
            copy.wait_send()

    w1a, w1b, w1c = {}, {}, {}
    for which in range(2):
        for h in range(2):
            key = (which, h)
            w1a[key] = phase_a(
                lambda hh, nx, ny, which=which: w1_one(which, hh, nx, ny),
                w1a_send.at[which, h], w1a_recv.at[which, h], h)
            w1b[key] = phase_b(
                lambda hh, n, which=which: w1_line(which, hh, n),
                w1b_send.at[which, h], w1b_recv.at[which, h], h)
            w1c[key] = phase_c(
                lambda hh, co, which=which: w1_plane(which, hh, co),
                w1c_send.at[which, h], w1c_recv.at[which, h], h)
    wga = [phase_a(wg_one, wga_send.at[h], wga_recv.at[h], h) for h in range(2)]
    wgb = [phase_b(wg_line, wgb_send.at[h], wgb_recv.at[h], h) for h in range(2)]
    wgc = [phase_c(wg_plane, wgc_send.at[h], wgc_recv.at[h], h) for h in range(2)]

    for h in range(2):
        start(w1a[0, h])
    for j in range(2, 6):
        for copy in kv[j]:
            copy.start()
    lax.fori_loop(1, 2, near, 0)
    for h in range(2):
        arrived(w1a[0, h])
        start(w1b[0, h])
    remote(w1.at[other_w, y, core], w1.at[other_w, y, core], wz_sem.at[0], wz_sem.at[1], far).wait_recv()
    for h in range(2):
        start(w1a[1, h])
    lax.fori_loop(2, 3, near, 0)
    for h in range(2):
        arrived(w1a[1, h])
        start(w1b[1, h])
    lax.fori_loop(3, 5, near, 0)
    for h in range(2):
        arrived(w1b[0, h])
        start(w1c[0, h])
    lax.fori_loop(5, 6, near, 0)
    for h in range(2):
        arrived(w1b[1, h])
        start(w1c[1, h])

    right = {"head": lax.rem(p + 1, NH)}
    left = {"head": lax.rem(p + NH - 1, NH)}

    def chain(way, k, q, src):
        return remote(src, buf.at[way, k, q], c_send.at[way, k, q], c_recv.at[way, k, q],
                      right if way == 0 else left)

    has_up = (p > 0, p < NH - 1)
    has_down = (p < NH - 1, p > 0)
    place = (p, NH - 1 - p)

    def finish(tile):
        for g in range(GROUP):
            i = tile * GROUP + g
            value = (acc[i] / l_s[i]).astype(BF)
            for q in range(2):
                ht[tile * 2 + q, g * HD:(g + 1) * HD, :] = value[:, q * 128:(q + 1) * 128]

    for which in range(2):
        for h in range(2):
            arrived(w1c[which, h])
    u = x * 8 + y * 2 + core
    uy, uc, uo = lax.div(u, 8), lax.rem(lax.div(u, 4), 2), lax.rem(u, 4) * 16
    wg[p, x, y, core] = w1[p, uy, uc, pl.ds(pl.multiple_of(uo, 16), 16)]

    def a2(n):
        peer, d = at_z(ring[n])
        return remote(
            w1.at[d, uy, uc, pl.ds(pl.multiple_of(uo, 16), 16)], wg.at[p, x, y, core],
            a2_send.at[n], a2_recv.at[n], peer)

    for n in range(len(ring)):
        a2(n).start()

    kv_wait(6)
    attend(6, 0)
    finish(0)
    for q in range(2):
        for way in range(2):
            @pl.when(has_down[way])
            def _():
                chain(way, 0, q, ht.at[q]).start()
    attend(6, 1)
    finish(1)

    def term(d, q):
        return jnp.dot(w1[d].reshape(512, 512), ht[2 + q], preferred_element_type=F32)

    def step(k, carry):
        for q in range(2):
            for way in range(2):
                slot = buf.at[way, k - 1, q]

                @pl.when(has_up[way])
                def _():
                    chain(way, k - 1, q, slot).wait_recv()

                adds = jnp.logical_and(k > place[way], has_down[way])
                far_place = NH + place[way] - k
                d = far_place if way == 0 else NH - 1 - far_place

                @pl.when(jnp.logical_and(adds, has_up[way]))
                def _():
                    slot[...] = (slot[...].astype(F32) + term(d, q)).astype(BF)

                @pl.when(jnp.logical_and(adds, jnp.logical_not(has_up[way])))
                def _():
                    slot[...] = term(d, q).astype(BF)

                @pl.when(has_down[way])
                def _():
                    chain(way, k, q, slot).start()
        return carry

    lax.fori_loop(1, 3, step, 0)
    for n in range(len(ring)):
        block = wg.at[at_z(-ring[n])[1], x, y, core]
        remote(block, block, a2_send.at[n], a2_recv.at[n], right).wait_recv()
    for h in range(2):
        start(wga[h])
    lax.fori_loop(3, 4, step, 0)
    for h in range(2):
        arrived(wga[h])
        start(wgb[h])
    lax.fori_loop(4, 6, step, 0)
    for h in range(2):
        arrived(wgb[h])
        start(wgc[h])
    lax.fori_loop(6, 8, step, 0)

    for h in range(2):
        arrived(wgc[h])
    for q in range(2):
        og[q] = jnp.dot(wg[p].reshape(512, 512), ht[q], preferred_element_type=F32)

    def gathered(h, carry):
        for q in range(2):
            @pl.when(h < p)
            def _():
                og[q] += jnp.dot(wg[h].reshape(512, 512), buf[0, p - 1 - h, q], preferred_element_type=F32)

            @pl.when(h > p)
            def _():
                og[q] += jnp.dot(wg[h].reshape(512, 512), buf[1, h - p - 1, q], preferred_element_type=F32)
        return carry

    lax.fori_loop(0, NH, gathered, 0)
    for q in range(2):
        o_ref[q * 128:(q + 1) * 128, :] = og[q].T.astype(BF)
    for q in range(2):
        og[q] = term(p, q)
    for q in range(2):
        for way in range(2):
            @pl.when(has_up[way])
            def _():
                chain(way, NH - 1, q, ht.at[q]).wait_recv()
                og[q] += buf[way, NH - 1, q].astype(F32)
        o_ref[256 + q * 128:256 + (q + 1) * 128, :] = og[q].T.astype(BF)

    for q in range(2):
        for way in range(2):
            @pl.when(has_down[way])
            def _():
                for k in range(NH):
                    chain(way, k, q, ht.at[q]).wait_send()
    wz.wait_send()
    for j in range(1, 7):
        for copy in kv[j]:
            copy.wait_send()
    for which in range(2):
        for h in range(2):
            sent(w1a[which, h])
            sent(w1b[which, h])
            sent(w1c[which, h])
    for n in range(len(ring)):
        a2(n).wait_send()
    for h in range(2):
        sent(wga[h])
        sent(wgb[h])
        sent(wgc[h])


def shards(query_rows, key_rows, value_rows, out_weight):
    dma = pltpu.SemaphoreType.DMA
    vmem = pl.BlockSpec(memory_space=pltpu.VMEM)
    return pl.pallas_call(
        kernel,
        out_shape=jax.ShapeDtypeStruct((BLOCK, GROUP * HD), BF),
        in_specs=[pl.BlockSpec(memory_space=pltpu.HBM)] * 4,
        out_specs=vmem,
        scratch_shapes=[
            pltpu.VMEM((BLOCK, GROUP * HD), BF),
            pltpu.VMEM((BLOCK, HD), BF),
            pltpu.VMEM((8, HD, 256), BF),
            pltpu.VMEM((7, BLOCK, HD), BF),
            pltpu.VMEM((7, HD, BLOCK), BF),
            pltpu.VMEM((8, 1, 256), F32),
            pltpu.VMEM((8, 1, 256), F32),
            pltpu.VMEM((8, HD, 256), F32),
            pltpu.VMEM((4, 512, 128), BF),
            pltpu.VMEM((8, 4, 2, 64, 512), BF),
            pltpu.VMEM((8, 4, 4, 2, 16, 512), BF),
            pltpu.VMEM((2, 8, 2, 512, 128), BF),
            pltpu.VMEM((2, 512, 128), F32),
            dma((4,)),
            dma((6,)), dma((6,)), dma((6,)), dma((6,)),
            dma((2,)),
            dma((2, 2, 3)), dma((2, 2, 3)), dma((2, 2, 3)), dma((2, 2, 3)), dma((2, 2)), dma((2, 2)),
            dma((7,)), dma((7,)),
            dma((2, 3)), dma((2, 3)), dma((2, 3)), dma((2, 3)), dma((2,)), dma((2,)),
            dma((2, 8, 2)), dma((2, 8, 2)),
        ],
        compiler_params=pltpu.CompilerParams(
            collective_id=0, has_side_effects=True, vmem_limit_bytes=60 * 1024 * 1024
        ),
        cost_estimate=pl.CostEstimate(flops=6_000_000_000, bytes_accessed=2_000_000, transcendentals=7_400_000),
    )(query_rows, key_rows, value_rows, out_weight.T)


def solution(mesh):
    placed = (P("ctx", "head"), P("ctx", "head"), P("ctx", "head"), P("head", "ctx"))
    return jax.shard_map(
        shards, mesh=mesh, in_specs=placed, out_specs=P("ctx", "head"), check_vma=False
    )
```
